32 devices in a mesh: dom: 16 (over z, y, core), section: 2 (over x).
Axes of the slice: x: 2, y: 2, z: 4, core: 2. Of those that a mesh axis runs over, the one named last changes fastest.
Arguments:
- feats: bfloat16 [65536, 1024], P('dom', 'section'), may hold values from -6 to 6
- tile_vals: bfloat16 [4096, 128, 128], P('dom'), may hold values from -0.1875 to 0.1875
- src_slot: int32 [4096], P('dom'), may hold values from 0 to 47, as said below
- dst_tile: int32 [4096], P('dom'), may hold values from 0 to 31
- tile_count: int32 [16], P('dom'), may hold values from 128 to 256, as said below
- send_tile: int32 [16, 48], P('dom'), may hold values from 0 to 31
- w_fwd: bfloat16 [1024, 1024], replicated, may hold values from -0.1875 to 0.1875
- b_fwd: float32 [1024], replicated, may hold values from -3 to 3
- w_inv1: bfloat16 [1024, 1024], replicated, may hold values from -0.1875 to 0.1875
- b_inv1: float32 [1024], replicated, may hold values from -3 to 3
- w_inv2: bfloat16 [1024, 1024], replicated, may hold values from -0.1875 to 0.1875
- b_inv2: float32 [1024], replicated, may hold values from -3 to 3
- target: bfloat16 [65536, 1024], P(('dom', 'section')), may hold values from -2.5 to 2.5
Outputs:
- hidden: bfloat16 [65536, 1024], P(('dom', 'section'))
- target_prev: bfloat16 [65536, 1024], P(('dom', 'section'))
The draws below stay inside these ranges and needn't reach their ends.
Inputs may be any that keep to these rules, and one draw needn't show every extreme that they name: `src_slot`: slots are numbered by sending partition, 3 each; in each partition's list the entry i names slot number pi(i mod 48) for a permutation pi of the partition. `tile_count`: some partition's list is full.
All inputs are finite; a program needn't handle non-finite values.
Results may differ from the reference program's by a relative error of at most 0.0042.
Values may be sent and summed in bfloat16 or wider, within the bound.
A program may use at most 192 MiB of HBM per device.

```python
import jax
import jax.numpy as jnp
from jax import lax

D = 1024
TILE = 128
ROWTILES = 32
SLOT = 3
NODES = 65536
LIST = 256
RECV = 48
N_DOM = 16


def draw_src_slot(key, part):
    keys = jax.random.split(key, N_DOM)

    def one_list(single_key):
        order = jax.random.permutation(single_key, RECV)
        return order[jnp.arange(LIST) % RECV]
    return jax.vmap(one_list)(keys).reshape(-1).astype(jnp.int32)


def draw_tile_count(key, part):
    first_key, second_key = jax.random.split(key)
    counts = jax.random.randint(first_key, (N_DOM,), LIST // 2, LIST + 1)
    full_index = jax.random.randint(second_key, (), 0, N_DOM)
    return jnp.where(jnp.arange(N_DOM) == full_index, LIST, counts).astype(jnp.int32)


def place_ends(entries, stream_key, low, high):
    dims = entries.shape
    place = [jax.random.randint(jax.random.fold_in(stream_key, axis), (), 0, dims[axis]) for axis in range(len(dims))]
    entries = entries.at[tuple(place)].set(low)
    longest = dims.index(max(dims))
    place[longest] = (place[longest] + 1) % dims[longest]
    return entries.at[tuple(place)].set(high)


def levels(key, extent, shards, low, high):
    def one(axis_at, parts):
        draws = jax.random.uniform(jax.random.fold_in(jax.random.fold_in(key, 6), axis_at), (parts,), jnp.float32, low / len(shards), high / len(shards))
        return jnp.repeat(jnp.exp(draws), extent[axis_at] // parts).reshape((-1,) + (1,) * (len(extent) - axis_at - 1))

    loudness = one(*shards[0])
    for cut in shards[1:]:
        loudness = loudness * one(*cut)
    return loudness


def bell_draw(own_key, dims, deviation, limit, shards=(), kind=jnp.bfloat16):
    drawn = jax.random.normal(own_key, dims, jnp.float32) * deviation
    if len(shards) > 0:
        drawn = levels(own_key, dims, shards, -0.22, 0.18) * drawn
    return jnp.clip(drawn, min=-limit, max=limit).astype(kind)


def setup_inputs(seed: int = 0) -> dict:
    key_of = jax.random.split(jax.random.key(seed), 14)
    return {
        "feats": bell_draw(key_of[0], (NODES, D), 1.0, 6.0, ((0, 16), (1, 2))),
        "tile_vals": bell_draw(key_of[1], (N_DOM * LIST, TILE, TILE), (8 * TILE) ** -0.5, 0.1875, ((0, 16),)),
        "src_slot": draw_src_slot(jax.random.fold_in(key_of[13], 71), 0),
        "dst_tile": place_ends(jax.random.randint(key_of[3], (N_DOM * LIST,), 0, ROWTILES), jax.random.fold_in(key_of[3], 1), 0, ROWTILES - 1).astype(jnp.int32),
        "tile_count": draw_tile_count(jax.random.fold_in(key_of[13], 71), 0),
        "send_tile": place_ends(jax.random.randint(key_of[5], (N_DOM, RECV), 0, ROWTILES), jax.random.fold_in(key_of[5], 1), 0, ROWTILES - 1).astype(jnp.int32),
        "w_fwd": bell_draw(key_of[6], (D, D), D ** -0.5, 0.1875),
        "b_fwd": bell_draw(key_of[7], (D,), 0.5, 3.0, (), jnp.float32),
        "w_inv1": bell_draw(key_of[8], (D, D), D ** -0.5, 0.1875),
        "b_inv1": bell_draw(key_of[9], (D,), 0.5, 3.0, (), jnp.float32),
        "w_inv2": bell_draw(key_of[10], (D, D), D ** -0.5, 0.1875),
        "b_inv2": bell_draw(key_of[11], (D,), 0.5, 3.0, (), jnp.float32),
        "target": bell_draw(key_of[12], (NODES, D), 0.6, 2.5, ((0, 32),)),
    }


def reference(feats, tile_vals, src_slot, dst_tile, tile_count, send_tile, w_fwd, b_fwd, w_inv1, b_inv1, w_inv2, b_inv2, target):
    flat_blocks = feats.reshape(N_DOM * ROWTILES, TILE, D)

    def one_part(part_index):
        my_slots = lax.dynamic_slice_in_dim(send_tile, part_index * SLOT, SLOT, 1).astype(jnp.int32)
        owners = jnp.arange(N_DOM, dtype=jnp.int32)[:, None] * ROWTILES + my_slots
        received = flat_blocks[owners.reshape(-1)]
        values_part = lax.dynamic_slice_in_dim(tile_vals, part_index * LIST, LIST, 0)
        slot_part = lax.dynamic_slice_in_dim(src_slot, part_index * LIST, LIST, 0)
        dest_part = lax.dynamic_slice_in_dim(dst_tile, part_index * LIST, LIST, 0)
        live_count = lax.dynamic_slice_in_dim(tile_count, part_index, 1, 0)[0]
        products = jnp.einsum("lab,lbc->lac", values_part.astype(jnp.float32), received[slot_part].astype(jnp.float32), precision=lax.Precision.HIGHEST)
        active = jnp.arange(LIST, dtype=jnp.int32) < live_count
        onehot = ((dest_part[None, :] == jnp.arange(ROWTILES, dtype=jnp.int32)[:, None]) & active[None, :]).astype(jnp.float32)
        summed = jnp.dot(onehot, products.reshape(LIST, TILE * D), precision=lax.Precision.HIGHEST)
        return summed.reshape(ROWTILES * TILE, D).astype(jnp.bfloat16)

    agg = lax.map(one_part, jnp.arange(N_DOM, dtype=jnp.int32)).reshape(N_DOM * ROWTILES * TILE, D)
    hidden = jnp.tanh(jnp.dot(agg, w_fwd, preferred_element_type=jnp.float32) + b_fwd).astype(jnp.bfloat16)

    def inverse(values):
        inner = jnp.tanh(jnp.dot(values, w_inv1, preferred_element_type=jnp.float32) + b_inv1).astype(jnp.bfloat16)
        return jnp.tanh(jnp.dot(inner, w_inv2, preferred_element_type=jnp.float32) + b_inv2)

    shifted = feats.astype(jnp.float32) + inverse(target) - inverse(hidden)
    return hidden, shifted.astype(jnp.bfloat16)
```

```python
import functools

import jax
import jax.numpy as jnp
from jax import lax
from jax.experimental import pallas as pl
from jax.experimental.pallas import tpu as pltpu
from jax.sharding import PartitionSpec as P

MESH = pl.DeviceIdType.MESH
BF16 = jnp.bfloat16
F32 = jnp.float32


def plan_kernel(steps, row_tiles, count_ref, dst_ref, slot_ref, plan_ref):
    entries = dst_ref.shape[1]
    width = plan_ref.shape[1]
    lane = lax.broadcasted_iota(jnp.int32, (entries, entries), 1)
    sub = lax.broadcasted_iota(jnp.int32, (entries, entries), 0)
    live = lax.broadcasted_iota(jnp.int32, (1, entries), 1) < count_ref[0]
    key_row = jnp.where(live, dst_ref[...], row_tiles).astype(F32)
    eye = lane == sub

    def column(row):
        return jnp.sum(jnp.where(eye, row, 0.0), axis=1, keepdims=True)

    key_col = column(key_row)
    slot_col = column(slot_ref[...].astype(F32))
    rank = jnp.sum(jnp.where((key_row == key_col) & (lane < sub), 1.0, 0.0), axis=1, keepdims=True)
    tile_lane = lax.broadcasted_iota(jnp.int32, (entries, width), 1).astype(F32)
    tile_sub = lax.broadcasted_iota(jnp.int32, (width, entries), 0).astype(F32)
    n_row = jnp.sum(jnp.where(key_col == tile_lane, 1.0, 0.0), axis=0, keepdims=True)
    n_col = jnp.sum(jnp.where(key_row == tile_sub, 1.0, 0.0), axis=1, keepdims=True)
    r_row = lax.broadcasted_iota(jnp.int32, (1, width), 1).astype(F32)
    r_col = lax.broadcasted_iota(jnp.int32, (width, 1), 0).astype(F32)
    pairs_row = jnp.where(r_row < row_tiles, jnp.floor((n_row + 1.0) * 0.5), 0.0)
    pairs_col = jnp.where(r_col < row_tiles, jnp.floor((n_col + 1.0) * 0.5), 0.0)
    big_lane = lax.broadcasted_iota(jnp.int32, (width, width), 1).astype(F32)
    big_sub = lax.broadcasted_iota(jnp.int32, (width, width), 0).astype(F32)
    start_row = jnp.sum(jnp.where(big_sub < big_lane, pairs_col, 0.0), axis=0, keepdims=True)
    start_col = jnp.sum(jnp.where(big_lane < big_sub, pairs_row, 0.0), axis=1, keepdims=True)
    start_of = jnp.sum(jnp.where(tile_lane < key_col, pairs_row, 0.0), axis=1, keepdims=True)
    place = jnp.where(key_col < row_tiles, 2.0 * start_of + rank, -1.0)
    entry_col = lax.broadcasted_iota(jnp.int32, (entries, 1), 0).astype(F32)
    for half in range(2):
        hit = place == 2.0 * tile_lane + float(half)
        found = jnp.sum(jnp.where(hit, 1.0, 0.0), axis=0, keepdims=True)
        entry = jnp.sum(jnp.where(hit, entry_col, 0.0), axis=0, keepdims=True)
        entry = entry + (1.0 - found) * float(entries)
        slot = jnp.sum(jnp.where(hit, slot_col, 0.0), axis=0, keepdims=True)
        plan_ref[half : half + 1, :] = entry.astype(jnp.int32)
        plan_ref[2 + half : 3 + half, :] = slot.astype(jnp.int32)
    opens = jnp.sum(
        jnp.where((start_col == big_lane) & (pairs_col > 0.0), 1.0, 0.0), axis=0, keepdims=True
    )
    plan_ref[4:5, :] = (1.0 - opens).astype(jnp.int32)
    last = jnp.where(pairs_row > 0.0, start_row + pairs_row - 1.0, float(steps))
    plan_ref[5:6, :] = last.astype(jnp.int32)
    plan_ref[6:8, :] = jnp.zeros((2, width), jnp.int32)


def layer_kernel(
    cfg,
    send_tile,
    plan,
    feats_hbm,
    vals_hbm,
    target_hbm,
    w_fwd_hbm,
    w_inv1_hbm,
    w_inv2_hbm,
    b_fwd,
    b_inv1,
    b_inv2,
    hidden_hbm,
    prev_hbm,
    feats,
    vals,
    target,
    w_fwd,
    w_inv1,
    w_inv2,
    whole_feats,
    base,
    agg,
    agg_out,
    sums,
    load_sem,
    out_sem,
    dom_send,
    dom_recv,
    feat_send,
    feat_recv,
    agg_send,
    agg_recv,
    *chunk_bufs,
):
    n, n_sec, slots, chunks, width, steps, group = cfg
    outgoing, received = chunk_bufs[:chunks], chunk_bufs[chunks:]
    me = lax.axis_index("dom")
    sec = lax.axis_index("section")
    row_tiles, side, cols = feats.shape
    own_tiles = row_tiles // n_sec
    groups = own_tiles // group
    entries = vals_hbm.shape[0]
    d = agg.shape[2]
    my_cols = pl.multiple_of(sec * cols, 128)

    loads = [
        pltpu.make_async_copy(feats_hbm, feats, load_sem.at[0]),
        pltpu.make_async_copy(target_hbm, target, load_sem.at[1]),
        pltpu.make_async_copy(w_inv1_hbm, w_inv1, load_sem.at[2]),
        pltpu.make_async_copy(w_inv2_hbm, w_inv2, load_sem.at[3]),
        pltpu.make_async_copy(vals_hbm, vals.at[pl.ds(0, entries)], load_sem.at[4]),
        pltpu.make_async_copy(w_fwd_hbm, w_fwd, load_sem.at[5]),
    ]
    for load in loads:
        load.start()

    barrier = pltpu.get_barrier_semaphore()

    def greet_dom(i, _):
        pl.semaphore_signal(
            barrier, inc=1, device_id=(lax.rem(me + i, n), sec), device_id_type=MESH
        )
        return 0

    def greet_sec(i, _):
        pl.semaphore_signal(
            barrier, inc=1, device_id=(me, lax.rem(sec + i, n_sec)), device_id_type=MESH
        )
        return 0

    lax.fori_loop(1, n, greet_dom, 0)
    lax.fori_loop(1, n_sec, greet_sec, 0)

    def offset(i):
        return n // 2 + (1 - 2 * lax.rem(i, 2)) * ((i + 1) // 2)

    def dom_copy(c, i):
        far = offset(i)
        return pltpu.make_async_remote_copy(
            src_ref=outgoing[c].at[pl.ds(i * slots, slots)],
            dst_ref=received[c].at[pl.ds(me * slots, slots)],
            send_sem=dom_send.at[c, i],
            recv_sem=dom_recv.at[c, i],
            device_id=(lax.rem(me + far, n), sec),
            device_id_type=MESH,
        )

    def dom_arrival(c, i):
        source = lax.rem(me + n - offset(i), n)
        return pltpu.make_async_remote_copy(
            src_ref=outgoing[c].at[pl.ds(i * slots, slots)],
            dst_ref=received[c].at[pl.ds(source * slots, slots)],
            send_sem=dom_send.at[c, i],
            recv_sem=dom_recv.at[c, i],
            device_id=(source, sec),
            device_id_type=MESH,
        )

    def feat_copy(i):
        other = lax.rem(sec + i, n_sec)
        return pltpu.make_async_remote_copy(
            src_ref=feats.at[pl.ds(other * own_tiles, own_tiles)],
            dst_ref=whole_feats.at[:, :, pl.ds(my_cols, cols)],
            send_sem=feat_send.at[i],
            recv_sem=feat_recv.at[i],
            device_id=(me, other),
            device_id_type=MESH,
        )

    def feat_arrival(i):
        source = lax.rem(sec + n_sec - i, n_sec)
        return pltpu.make_async_remote_copy(
            src_ref=feats.at[pl.ds(source * own_tiles, own_tiles)],
            dst_ref=whole_feats.at[:, :, pl.ds(pl.multiple_of(source * cols, 128), cols)],
            send_sem=feat_send.at[i],
            recv_sem=feat_recv.at[i],
            device_id=(me, source),
            device_id_type=MESH,
        )

    def agg_copy(c, i, b):
        other = lax.rem(sec + i, n_sec)
        return pltpu.make_async_remote_copy(
            src_ref=agg_out.at[c, i - 1, pl.ds(b * group, group)],
            dst_ref=agg.at[
                pl.ds(b * group, group),
                :,
                pl.ds(pl.multiple_of(my_cols + c * width, 128), width),
            ],
            send_sem=agg_send.at[c, i, b],
            recv_sem=agg_recv.at[c, i, b],
            device_id=(me, other),
            device_id_type=MESH,
        )

    def agg_arrival(c, i, b):
        source = lax.rem(sec + n_sec - i, n_sec)
        return pltpu.make_async_remote_copy(
            src_ref=agg_out.at[c, i - 1, pl.ds(b * group, group)],
            dst_ref=agg.at[
                pl.ds(b * group, group),
                :,
                pl.ds(pl.multiple_of(source * cols + c * width, 128), width),
            ],
            send_sem=agg_send.at[c, i, b],
            recv_sem=agg_recv.at[c, i, b],
            device_id=(me, source),
            device_id_type=MESH,
        )

    loads[0].wait()
    own_feats = pltpu.make_async_copy(
        feats.at[pl.ds(sec * own_tiles, own_tiles)],
        whole_feats.at[:, :, pl.ds(my_cols, cols)],
        load_sem.at[6],
    )
    own_feats.start()
    for c in range(chunks):
        left = slice(c * width, (c + 1) * width)

        def gather(i, _):
            first = lax.rem(me + offset(i), n) * slots
            for k in range(slots):
                outgoing[c][i * slots + k] = feats[send_tile[0, first + k], :, left]
            return 0

        lax.fori_loop(0, n - 1, gather, 0)
        for k in range(slots):
            received[c][me * slots + k] = feats[send_tile[0, me * slots + k], :, left]
        if c == 0:
            pl.semaphore_wait(barrier, n + n_sec - 2)

        def send(i, _):
            dom_copy(c, i).start()
            return 0

        lax.fori_loop(0, n - 1, send, 0)

    def send_feat(i, _):
        feat_copy(i).start()
        return 0

    lax.fori_loop(1, n_sec, send_feat, 0)

    def inverse(values):
        inner = jnp.tanh(
            jnp.dot(values, w_inv1[...], preferred_element_type=F32) + b_inv1[...]
        ).astype(BF16)
        return jnp.tanh(jnp.dot(inner, w_inv2[...], preferred_element_type=F32) + b_inv2[...])

    for load in loads[1:4]:
        load.wait()

    def target_block(b, _):
        rows = pl.ds(b * group, group)
        values = target[rows].reshape(group * side, d)
        base[rows] = inverse(values).reshape(group, side, d)
        return 0

    lax.fori_loop(0, groups, target_block, 0)

    vals[entries] = jnp.zeros((side, side), BF16)
    sums[steps] = jnp.zeros((side, width), BF16)
    loads[4].wait()

    for c in range(chunks):

        def arrive(i, _):
            dom_arrival(c, i).wait_recv()
            return 0

        lax.fori_loop(0, n - 1, arrive, 0)

        def step(t, total):
            left = jnp.concatenate([vals[plan[0, t]], vals[plan[1, t]]], axis=1)
            right = jnp.concatenate(
                [received[c][plan[2, t]], received[c][plan[3, t]]], axis=0
            )
            total = total * plan[4, t].astype(F32) + jnp.dot(
                left, right, preferred_element_type=F32
            )
            sums[t] = total.astype(BF16)
            return total

        unroll = 4 if steps % 4 == 0 else 1

        def several(t, total):
            for u in range(unroll):
                total = step(t * unroll + u, total)
            return total

        lax.fori_loop(0, steps // unroll, several, jnp.zeros((side, width), F32))

        def hand_out(b, _):
            for i in range(1, n_sec):
                first = lax.rem(sec + i, n_sec) * own_tiles + b * group
                for k in range(group):
                    agg_out[c, i - 1, b * group + k] = sums[plan[5, first + k]]
                agg_copy(c, i, b).start()
            return 0

        lax.fori_loop(0, groups, hand_out, 0)

        def keep_own(b, _):
            agg[b, :, pl.ds(pl.multiple_of(my_cols + c * width, 128), width)] = sums[
                plan[5, sec * own_tiles + b]
            ]
            return 0

        lax.fori_loop(0, own_tiles, keep_own, 0)

    loads[5].wait()
    own_feats.wait()

    def feat_in(i, _):
        feat_arrival(i).wait_recv()
        return 0

    lax.fori_loop(1, n_sec, feat_in, 0)

    def out_copies(b):
        rows = pl.ds(b * group, group)
        return (
            pltpu.make_async_copy(agg.at[rows], hidden_hbm.at[rows], out_sem.at[0, b]),
            pltpu.make_async_copy(target.at[rows], prev_hbm.at[rows], out_sem.at[1, b]),
        )

    def hidden_block(b, _):
        for c in range(chunks):
            for i in range(1, n_sec):
                agg_arrival(c, i, b).wait_recv()
        rows = pl.ds(b * group, group)
        values = agg[rows].reshape(group * side, d)
        hidden = jnp.tanh(
            jnp.dot(values, w_fwd[...], preferred_element_type=F32) + b_fwd[...]
        ).astype(BF16)
        agg[rows] = hidden.reshape(group, side, d)
        out_copies(b)[0].start()
        back = inverse(hidden).reshape(group, side, d)
        shifted = whole_feats[rows].astype(F32) + base[rows] - back
        target[rows] = shifted.astype(BF16)
        out_copies(b)[1].start()
        return 0

    lax.fori_loop(0, groups, hidden_block, 0)

    def finish(b, _):
        for copy in out_copies(b):
            copy.wait()
        for c in range(chunks):
            for i in range(1, n_sec):
                agg_copy(c, i, b).wait_send()
        return 0

    lax.fori_loop(0, groups, finish, 0)

    def sent_feat(i, _):
        feat_copy(i).wait_send()
        return 0

    lax.fori_loop(1, n_sec, sent_feat, 0)

    def sent_dom(i, _):
        for c in range(chunks):
            dom_copy(c, i).wait_send()
        return 0

    lax.fori_loop(0, n - 1, sent_dom, 0)


def per_device(
    n,
    n_sec,
    feats,
    tile_vals,
    src_slot,
    dst_tile,
    tile_count,
    send_tile,
    w_fwd,
    b_fwd,
    w_inv1,
    b_inv1,
    w_inv2,
    b_inv2,
    target,
):
    node_rows, cols = feats.shape
    entries, side, _ = tile_vals.shape
    row_tiles = node_rows // side
    own_tiles = row_tiles // n_sec
    slots = send_tile.shape[1] // n
    d = w_fwd.shape[0]
    width = 128 if cols % 128 == 0 else cols
    chunks = cols // width
    steps = (entries + row_tiles + 1) // 2
    steps = (steps + 3) // 4 * 4
    plan_width = (max(steps, row_tiles) + 127) // 128 * 128
    group = 2 if own_tiles % 2 == 0 else 1
    groups = own_tiles // group
    smem = pl.BlockSpec(memory_space=pltpu.SMEM)
    vmem = pl.BlockSpec(memory_space=pltpu.VMEM)
    hbm = pl.BlockSpec(memory_space=pl.ANY)

    plan = pl.pallas_call(
        functools.partial(plan_kernel, steps, row_tiles),
        out_shape=jax.ShapeDtypeStruct((8, plan_width), jnp.int32),
        in_specs=[smem, vmem, vmem],
        out_specs=vmem,
    )(tile_count, dst_tile.reshape(1, entries), src_slot.reshape(1, entries))

    cfg = (n, n_sec, slots, chunks, width, steps, group)
    rows_shape = (own_tiles, side, d)
    dma = pltpu.SemaphoreType.DMA
    scratch = [
        pltpu.VMEM((row_tiles, side, cols), BF16),
        pltpu.VMEM((entries + 1, side, side), BF16),
        pltpu.VMEM(rows_shape, BF16),
        pltpu.VMEM((d, d), BF16),
        pltpu.VMEM((d, d), BF16),
        pltpu.VMEM((d, d), BF16),
        pltpu.VMEM(rows_shape, BF16),
        pltpu.VMEM(rows_shape, F32),
        pltpu.VMEM(rows_shape, BF16),
        pltpu.VMEM((chunks, n_sec - 1, own_tiles, side, width), BF16),
        pltpu.VMEM((steps + 1, side, width), BF16),
        dma((7,)),
        dma((2, groups)),
        dma((chunks, n - 1)),
        dma((chunks, n - 1)),
        dma((n_sec,)),
        dma((n_sec,)),
        dma((chunks, n_sec, groups)),
        dma((chunks, n_sec, groups)),
    ]
    scratch += [pltpu.VMEM(((n - 1) * slots, side, width), BF16) for _ in range(chunks)]
    scratch += [pltpu.VMEM((n * slots, side, width), BF16) for _ in range(chunks)]
    hidden, prev = pl.pallas_call(
        functools.partial(layer_kernel, cfg),
        out_shape=[jax.ShapeDtypeStruct(rows_shape, BF16)] * 2,
        in_specs=[smem, smem] + [hbm] * 6 + [vmem] * 3,
        out_specs=[hbm, hbm],
        scratch_shapes=scratch,
        compiler_params=pltpu.CompilerParams(
            collective_id=0, has_side_effects=True, vmem_limit_bytes=63 * 1024 * 1024
        ),
    )(
        send_tile,
        plan,
        feats.reshape(row_tiles, side, cols),
        tile_vals,
        target.reshape(rows_shape),
        w_fwd,
        w_inv1,
        w_inv2,
        b_fwd.reshape(1, d),
        b_inv1.reshape(1, d),
        b_inv2.reshape(1, d),
    )
    return hidden.reshape(target.shape), prev.reshape(target.shape)


def solution(mesh):
    placed = (
        P("dom", "section"),
        P("dom", None, None),
        P("dom"),
        P("dom"),
        P("dom"),
        P("dom", None),
        P(),
        P(),
        P(),
        P(),
        P(),
        P(),
        P(("dom", "section"), None),
    )
    return jax.shard_map(
        functools.partial(per_device, mesh.shape["dom"], mesh.shape["section"]),
        mesh=mesh,
        in_specs=placed,
        out_specs=(P(("dom", "section"), None), P(("dom", "section"), None)),
        check_vma=False,
    )
```

```python
import functools

import jax
import jax.numpy as jnp
from jax import lax
from jax.experimental import pallas as pl
from jax.experimental.pallas import tpu as pltpu
from jax.sharding import PartitionSpec as P

MESH = pl.DeviceIdType.MESH
BF16 = jnp.bfloat16
F32 = jnp.float32


def plan_kernel(steps, row_tiles, count_ref, dst_ref, slot_ref, plan_ref):
    entries = dst_ref.shape[1]
    width = plan_ref.shape[1]
    lane = lax.broadcasted_iota(jnp.int32, (entries, entries), 1)
    sub = lax.broadcasted_iota(jnp.int32, (entries, entries), 0)
    live = lax.broadcasted_iota(jnp.int32, (1, entries), 1) < count_ref[0]
    key_row = jnp.where(live, dst_ref[...], row_tiles).astype(F32)
    eye = lane == sub

    def column(row):
        return jnp.sum(jnp.where(eye, row, 0.0), axis=1, keepdims=True)

    key_col = column(key_row)
    slot_col = column(slot_ref[...].astype(F32))
    rank = jnp.sum(jnp.where((key_row == key_col) & (lane < sub), 1.0, 0.0), axis=1, keepdims=True)
    tile_lane = lax.broadcasted_iota(jnp.int32, (entries, width), 1).astype(F32)
    tile_sub = lax.broadcasted_iota(jnp.int32, (width, entries), 0).astype(F32)
    n_row = jnp.sum(jnp.where(key_col == tile_lane, 1.0, 0.0), axis=0, keepdims=True)
    n_col = jnp.sum(jnp.where(key_row == tile_sub, 1.0, 0.0), axis=1, keepdims=True)
    r_row = lax.broadcasted_iota(jnp.int32, (1, width), 1).astype(F32)
    r_col = lax.broadcasted_iota(jnp.int32, (width, 1), 0).astype(F32)
    pairs_row = jnp.where(r_row < row_tiles, jnp.floor((n_row + 1.0) * 0.5), 0.0)
    pairs_col = jnp.where(r_col < row_tiles, jnp.floor((n_col + 1.0) * 0.5), 0.0)
    big_lane = lax.broadcasted_iota(jnp.int32, (width, width), 1).astype(F32)
    big_sub = lax.broadcasted_iota(jnp.int32, (width, width), 0).astype(F32)
    start_row = jnp.sum(jnp.where(big_sub < big_lane, pairs_col, 0.0), axis=0, keepdims=True)
    start_col = jnp.sum(jnp.where(big_lane < big_sub, pairs_row, 0.0), axis=1, keepdims=True)
    start_of = jnp.sum(jnp.where(tile_lane < key_col, pairs_row, 0.0), axis=1, keepdims=True)
    place = jnp.where(key_col < row_tiles, 2.0 * start_of + rank, -1.0)
    entry_col = lax.broadcasted_iota(jnp.int32, (entries, 1), 0).astype(F32)
    for half in range(2):
        hit = place == 2.0 * tile_lane + float(half)
        found = jnp.sum(jnp.where(hit, 1.0, 0.0), axis=0, keepdims=True)
        entry = jnp.sum(jnp.where(hit, entry_col, 0.0), axis=0, keepdims=True)
        entry = entry + (1.0 - found) * float(entries)
        slot = jnp.sum(jnp.where(hit, slot_col, 0.0), axis=0, keepdims=True)
        plan_ref[half : half + 1, :] = entry.astype(jnp.int32)
        plan_ref[2 + half : 3 + half, :] = slot.astype(jnp.int32)
    opens = jnp.sum(
        jnp.where((start_col == big_lane) & (pairs_col > 0.0), 1.0, 0.0), axis=0, keepdims=True
    )
    plan_ref[4:5, :] = (1.0 - opens).astype(jnp.int32)
    last = jnp.where(pairs_row > 0.0, start_row + pairs_row - 1.0, float(steps))
    plan_ref[5:6, :] = last.astype(jnp.int32)
    plan_ref[6:8, :] = jnp.zeros((2, width), jnp.int32)


def layer_kernel(
    cfg,
    send_tile,
    plan,
    feats_hbm,
    vals_hbm,
    target_hbm,
    w_fwd_hbm,
    w_inv1_hbm,
    w_inv2_hbm,
    b_fwd,
    b_inv1,
    b_inv2,
    hidden_hbm,
    prev_hbm,
    feats,
    vals,
    target,
    w_fwd,
    w_inv1,
    w_inv2,
    whole_feats,
    agg,
    agg_out,
    sums,
    load_sem,
    out_sem,
    dom_send,
    dom_recv,
    feat_send,
    feat_recv,
    agg_send,
    agg_recv,
    *chunk_bufs,
):
    n, n_sec, slots, chunks, width, steps, group = cfg
    outgoing, received = chunk_bufs[:chunks], chunk_bufs[chunks:]
    me = lax.axis_index("dom")
    sec = lax.axis_index("section")
    row_tiles, side, cols = feats.shape
    own_tiles = row_tiles // n_sec
    groups = own_tiles // group
    entries = vals_hbm.shape[0]
    d = agg.shape[2]
    my_cols = pl.multiple_of(sec * cols, 128)

    loads = [
        pltpu.make_async_copy(feats_hbm, feats, load_sem.at[0]),
        pltpu.make_async_copy(target_hbm, target, load_sem.at[1]),
        pltpu.make_async_copy(w_inv1_hbm, w_inv1, load_sem.at[2]),
        pltpu.make_async_copy(w_inv2_hbm, w_inv2, load_sem.at[3]),
        pltpu.make_async_copy(vals_hbm, vals.at[pl.ds(0, entries)], load_sem.at[4]),
        pltpu.make_async_copy(w_fwd_hbm, w_fwd, load_sem.at[5]),
    ]
    loads[0].start()

    barrier = pltpu.get_barrier_semaphore()

    def greet_dom(i, _):
        pl.semaphore_signal(
            barrier, inc=1, device_id=(lax.rem(me + i, n), sec), device_id_type=MESH
        )
        return 0

    def greet_sec(i, _):
        pl.semaphore_signal(
            barrier, inc=1, device_id=(me, lax.rem(sec + i, n_sec)), device_id_type=MESH
        )
        return 0

    lax.fori_loop(1, n, greet_dom, 0)
    lax.fori_loop(1, n_sec, greet_sec, 0)

    def offset(i):
        return n // 2 + (1 - 2 * lax.rem(i, 2)) * ((i + 1) // 2)

    def dom_copy(c, i):
        far = offset(i)
        return pltpu.make_async_remote_copy(
            src_ref=outgoing[c].at[pl.ds(i * slots, slots)],
            dst_ref=received[c].at[pl.ds(me * slots, slots)],
            send_sem=dom_send.at[c, i],
            recv_sem=dom_recv.at[c, i],
            device_id=(lax.rem(me + far, n), sec),
            device_id_type=MESH,
        )

    def dom_arrival(c, i):
        source = lax.rem(me + n - offset(i), n)
        return pltpu.make_async_remote_copy(
            src_ref=outgoing[c].at[pl.ds(i * slots, slots)],
            dst_ref=received[c].at[pl.ds(source * slots, slots)],
            send_sem=dom_send.at[c, i],
            recv_sem=dom_recv.at[c, i],
            device_id=(source, sec),
            device_id_type=MESH,
        )

    def feat_copy(i):
        other = lax.rem(sec + i, n_sec)
        return pltpu.make_async_remote_copy(
            src_ref=feats.at[pl.ds(other * own_tiles, own_tiles)],
            dst_ref=whole_feats.at[:, :, pl.ds(my_cols, cols)],
            send_sem=feat_send.at[i],
            recv_sem=feat_recv.at[i],
            device_id=(me, other),
            device_id_type=MESH,
        )

    def feat_arrival(i):
        source = lax.rem(sec + n_sec - i, n_sec)
        return pltpu.make_async_remote_copy(
            src_ref=feats.at[pl.ds(source * own_tiles, own_tiles)],
            dst_ref=whole_feats.at[:, :, pl.ds(pl.multiple_of(source * cols, 128), cols)],
            send_sem=feat_send.at[i],
            recv_sem=feat_recv.at[i],
            device_id=(me, source),
            device_id_type=MESH,
        )

    def agg_copy(c, i, b):
        other = lax.rem(sec + i, n_sec)
        return pltpu.make_async_remote_copy(
            src_ref=agg_out.at[c, i - 1, pl.ds(b * group, group)],
            dst_ref=agg.at[
                pl.ds(b * group, group),
                :,
                pl.ds(pl.multiple_of(my_cols + c * width, 128), width),
            ],
            send_sem=agg_send.at[c, i, b],
            recv_sem=agg_recv.at[c, i, b],
            device_id=(me, other),
            device_id_type=MESH,
        )

    def agg_arrival(c, i, b):
        source = lax.rem(sec + n_sec - i, n_sec)
        return pltpu.make_async_remote_copy(
            src_ref=agg_out.at[c, i - 1, pl.ds(b * group, group)],
            dst_ref=agg.at[
                pl.ds(b * group, group),
                :,
                pl.ds(pl.multiple_of(source * cols + c * width, 128), width),
            ],
            send_sem=agg_send.at[c, i, b],
            recv_sem=agg_recv.at[c, i, b],
            device_id=(me, source),
            device_id_type=MESH,
        )

    loads[0].wait()
    own_feats = pltpu.make_async_copy(
        feats.at[pl.ds(sec * own_tiles, own_tiles)],
        whole_feats.at[:, :, pl.ds(my_cols, cols)],
        load_sem.at[6],
    )
    own_feats.start()
    for c in range(chunks):
        left = slice(c * width, (c + 1) * width)

        def gather(i, _):
            first = lax.rem(me + offset(i), n) * slots
            for k in range(slots):
                outgoing[c][i * slots + k] = feats[send_tile[0, first + k], :, left]
            return 0

        lax.fori_loop(0, n - 1, gather, 0)
        for k in range(slots):
            received[c][me * slots + k] = feats[send_tile[0, me * slots + k], :, left]
        if c == 0:
            pl.semaphore_wait(barrier, n + n_sec - 2)

        def send(i, _):
            dom_copy(c, i).start()
            return 0

        lax.fori_loop(0, n - 1, send, 0)
        if c == 0:
            for load in loads[1:]:
                load.start()

    def send_feat(i, _):
        feat_copy(i).start()
        return 0

    lax.fori_loop(1, n_sec, send_feat, 0)

    def inverse(values):
        inner = jnp.tanh(
            jnp.dot(values, w_inv1[...], preferred_element_type=F32) + b_inv1[...]
        ).astype(BF16)
        return jnp.tanh(jnp.dot(inner, w_inv2[...], preferred_element_type=F32) + b_inv2[...])

    for load in loads[1:4]:
        load.wait()

    def target_block(b, _):
        rows = pl.ds(b * group, group)
        values = target[rows].reshape(group * side, d)
        target[rows] = inverse(values).astype(BF16).reshape(group, side, d)
        return 0

    lax.fori_loop(0, groups, target_block, 0)

    vals[entries] = jnp.zeros((side, side), BF16)
    sums[steps] = jnp.zeros((side, width), BF16)
    loads[4].wait()

    for c in range(chunks):

        def arrive(i, _):
            dom_arrival(c, i).wait_recv()
            return 0

        lax.fori_loop(0, n - 1, arrive, 0)

        def step(t, total):
            left = jnp.concatenate([vals[plan[0, t]], vals[plan[1, t]]], axis=1)
            right = jnp.concatenate(
                [received[c][plan[2, t]], received[c][plan[3, t]]], axis=0
            )
            total = total * plan[4, t].astype(F32) + jnp.dot(
                left, right, preferred_element_type=F32
            )
            sums[t] = total.astype(BF16)
            return total

        unroll = 4 if steps % 4 == 0 else 1

        def several(t, total):
            for u in range(unroll):
                total = step(t * unroll + u, total)
            return total

        lax.fori_loop(0, steps // unroll, several, jnp.zeros((side, width), F32))

        def hand_out(b, _):
            for i in range(1, n_sec):
                first = lax.rem(sec + i, n_sec) * own_tiles + b * group
                for k in range(group):
                    agg_out[c, i - 1, b * group + k] = sums[plan[5, first + k]]
                agg_copy(c, i, b).start()
            return 0

        lax.fori_loop(0, groups, hand_out, 0)

        def keep_own(b, _):
            agg[b, :, pl.ds(pl.multiple_of(my_cols + c * width, 128), width)] = sums[
                plan[5, sec * own_tiles + b]
            ]
            return 0

        lax.fori_loop(0, own_tiles, keep_own, 0)

    loads[5].wait()
    own_feats.wait()

    def feat_in(i, _):
        feat_arrival(i).wait_recv()
        return 0

    lax.fori_loop(1, n_sec, feat_in, 0)

    def out_copies(b):
        rows = pl.ds(b * group, group)
        return (
            pltpu.make_async_copy(agg.at[rows], hidden_hbm.at[rows], out_sem.at[0, b]),
            pltpu.make_async_copy(target.at[rows], prev_hbm.at[rows], out_sem.at[1, b]),
        )

    def hidden_block(b, _):
        for c in range(chunks):
            for i in range(1, n_sec):
                agg_arrival(c, i, b).wait_recv()
        rows = pl.ds(b * group, group)
        values = agg[rows].reshape(group * side, d)
        hidden = jnp.tanh(
            jnp.dot(values, w_fwd[...], preferred_element_type=F32) + b_fwd[...]
        ).astype(BF16)
        agg[rows] = hidden.reshape(group, side, d)
        out_copies(b)[0].start()
        back = inverse(hidden).reshape(group, side, d)
        shifted = whole_feats[rows].astype(F32) + target[rows].astype(F32) - back
        target[rows] = shifted.astype(BF16)
        out_copies(b)[1].start()
        return 0

    lax.fori_loop(0, groups, hidden_block, 0)

    def finish(b, _):
        for copy in out_copies(b):
            copy.wait()
        for c in range(chunks):
            for i in range(1, n_sec):
                agg_copy(c, i, b).wait_send()
        return 0

    lax.fori_loop(0, groups, finish, 0)

    def sent_feat(i, _):
        feat_copy(i).wait_send()
        return 0

    lax.fori_loop(1, n_sec, sent_feat, 0)

    def sent_dom(i, _):
        for c in range(chunks):
            dom_copy(c, i).wait_send()
        return 0

    lax.fori_loop(0, n - 1, sent_dom, 0)


def per_device(
    n,
    n_sec,
    feats,
    tile_vals,
    src_slot,
    dst_tile,
    tile_count,
    send_tile,
    w_fwd,
    b_fwd,
    w_inv1,
    b_inv1,
    w_inv2,
    b_inv2,
    target,
):
    node_rows, cols = feats.shape
    entries, side, _ = tile_vals.shape
    row_tiles = node_rows // side
    own_tiles = row_tiles // n_sec
    slots = send_tile.shape[1] // n
    d = w_fwd.shape[0]
    width = 256 if cols % 256 == 0 else 128
    chunks = cols // width
    steps = (entries + row_tiles + 1) // 2
    steps = (steps + 3) // 4 * 4
    plan_width = (max(steps, row_tiles) + 127) // 128 * 128
    group = 2 if own_tiles % 2 == 0 else 1
    groups = own_tiles // group
    smem = pl.BlockSpec(memory_space=pltpu.SMEM)
    vmem = pl.BlockSpec(memory_space=pltpu.VMEM)
    hbm = pl.BlockSpec(memory_space=pl.ANY)

    plan = pl.pallas_call(
        functools.partial(plan_kernel, steps, row_tiles),
        out_shape=jax.ShapeDtypeStruct((8, plan_width), jnp.int32),
        in_specs=[smem, vmem, vmem],
        out_specs=vmem,
    )(tile_count, dst_tile.reshape(1, entries), src_slot.reshape(1, entries))

    cfg = (n, n_sec, slots, chunks, width, steps, group)
    rows_shape = (own_tiles, side, d)
    dma = pltpu.SemaphoreType.DMA
    scratch = [
        pltpu.VMEM((row_tiles, side, cols), BF16),
        pltpu.VMEM((entries + 1, side, side), BF16),
        pltpu.VMEM(rows_shape, BF16),
        pltpu.VMEM((d, d), BF16),
        pltpu.VMEM((d, d), BF16),
        pltpu.VMEM((d, d), BF16),
        pltpu.VMEM(rows_shape, BF16),
        pltpu.VMEM(rows_shape, BF16),
        pltpu.VMEM((chunks, n_sec - 1, own_tiles, side, width), BF16),
        pltpu.VMEM((steps + 1, side, width), BF16),
        dma((7,)),
        dma((2, groups)),
        dma((chunks, n - 1)),
        dma((chunks, n - 1)),
        dma((n_sec,)),
        dma((n_sec,)),
        dma((chunks, n_sec, groups)),
        dma((chunks, n_sec, groups)),
    ]
    scratch += [pltpu.VMEM(((n - 1) * slots, side, width), BF16) for _ in range(chunks)]
    scratch += [pltpu.VMEM((n * slots, side, width), BF16) for _ in range(chunks)]
    hidden, prev = pl.pallas_call(
        functools.partial(layer_kernel, cfg),
        out_shape=[jax.ShapeDtypeStruct(rows_shape, BF16)] * 2,
        in_specs=[smem, smem] + [hbm] * 6 + [vmem] * 3,
        out_specs=[hbm, hbm],
        scratch_shapes=scratch,
        compiler_params=pltpu.CompilerParams(
            collective_id=0, has_side_effects=True, vmem_limit_bytes=63 * 1024 * 1024
        ),
    )(
        send_tile,
        plan,
        feats.reshape(row_tiles, side, cols),
        tile_vals,
        target.reshape(rows_shape),
        w_fwd,
        w_inv1,
        w_inv2,
        b_fwd.reshape(1, d),
        b_inv1.reshape(1, d),
        b_inv2.reshape(1, d),
    )
    return hidden.reshape(target.shape), prev.reshape(target.shape)


def solution(mesh):
    placed = (
        P("dom", "section"),
        P("dom", None, None),
        P("dom"),
        P("dom"),
        P("dom"),
        P("dom", None),
        P(),
        P(),
        P(),
        P(),
        P(),
        P(),
        P(("dom", "section"), None),
    )
    return jax.shard_map(
        functools.partial(per_device, mesh.shape["dom"], mesh.shape["section"]),
        mesh=mesh,
        in_specs=placed,
        out_specs=(P(("dom", "section"), None), P(("dom", "section"), None)),
        check_vma=False,
    )
```
